32 devices in a mesh: route: 16 (over z, y, x), scen: 2 (over core).
Axes of the slice: x: 2, y: 2, z: 4, core: 2. Of those that a mesh axis runs over, the one named last changes fastest.
Arguments:
- starting_warming: float32 [128, 16, 512], P('route', 'scen'), may hold values from -6 to 6
- schur_reciprocal: float32 [4, 512, 512], replicated, may hold values from -1 to 1
- ground_level_group: int32 [128], P('route'), may hold values from 0 to 3
- link_coefficient: float32 [128, 128], P('route'), may hold values from 40 to 16384
- dissipation_matrices: float32 [2, 128, 6, 512], P('scen', 'route'), may hold values from 0.05 to 1
- timestep_holder: int32 [2, 6], replicated, may hold values from 0 to 1
- current_demand: int32 [2, 6, 16], P(None, None, 'scen'), may hold values from 0 to 10
Outputs:
- temperatures: float32 [2, 128, 16, 512], P(None, 'route', 'scen')
The draws below stay inside these ranges and needn't reach their ends.
All inputs are finite; a program needn't handle non-finite values.
Results may differ from the reference program's by a relative error of at most 0.0042.
Values sent between devices are 32-bit elements; how exact they have to be, the bound alone decides.
A program may use at most 64 MiB of HBM per device.

```python
import math
import jax
import jax.numpy as jnp
from jax import lax

GRID_NODES = 512
CORE = 128
CIRCUITS = 6
CLASSES = 4
HOURS = 2
LINE_PIECES = 128
LOAD_CASES = 16
N_SCEN = 2


def core_profile(key):
    random_keys = jax.random.split(jax.random.fold_in(key, 11), 2)
    slow_cut = 5
    slow_segment_mask = jax.random.randint(random_keys[0], (CORE,), 0, 10) < slow_cut
    log_retain = jax.random.uniform(random_keys[1], (CORE,), jnp.float32, math.log(0.35), math.log(0.8))
    half_power = max((LINE_PIECES // 2 - 1).bit_length(), 0)
    slow_scale = 2.0 ** (-2 * half_power)
    scale = jnp.where(slow_segment_mask, slow_scale, 0.02).astype(jnp.float32)
    return (slow_segment_mask, log_retain, scale)


def draw_schur_reciprocal(key, part):
    slow_segment_mask, log_retain, scale = core_profile(key)
    first_key, second_key = jax.random.split(jax.random.fold_in(key, 3))
    spread = 0.3 / math.sqrt(GRID_NODES)
    mixing = 1.6 / (LINE_PIECES * math.sqrt(CORE))
    noise = jax.random.normal(first_key, (CLASSES, GRID_NODES, GRID_NODES), jnp.float32)
    noise = jnp.clip(noise, -6.0, 6.0)
    symmetric = (noise + jnp.swapaxes(noise, 1, 2)) * (1.0 / math.sqrt(2.0))
    segment_positions = jnp.arange(GRID_NODES)
    is_core = segment_positions < CORE
    line = jnp.concatenate([scale, jnp.ones((GRID_NODES - CORE,), jnp.float32)])
    both_core = is_core[:, None] & is_core[None, :]
    weights = jnp.where(both_core, mixing * jnp.sqrt(line[:, None] * line[None, :]), spread * line[:, None] * line[None, :])
    outer_diag = jax.random.uniform(second_key, (CLASSES, GRID_NODES), jnp.float32, 0.8, 1.0)
    diagonal = jnp.where(is_core[None, :], line[None, :], outer_diag)
    identity = jnp.eye(GRID_NODES, dtype=jnp.float32)
    table = symmetric * weights[None] * (1.0 - identity)[None] + identity[None] * diagonal[:, :, None]
    return table.astype(jnp.float32)


def draw_link_coefficient(key, part):
    slow_segment_mask, log_retain, scale = core_profile(key)
    random_keys = jax.random.split(jax.random.fold_in(key, 7), 3)
    jitter = jax.random.uniform(random_keys[0], (LINE_PIECES, CORE), jnp.float32, 0.5, 1.5)
    slow_retention = jnp.exp(log_retain[None, :] * jitter * (1.0 / LINE_PIECES))
    surge_rows = jax.random.randint(random_keys[1], (3,), 0, LINE_PIECES)
    segment_positions = jnp.arange(LINE_PIECES)
    is_surging = jnp.any(segment_positions[:, None] == surge_rows[None, :], axis=1)
    surge_factor = jnp.where(is_surging, 0.7, 1.0).astype(jnp.float32)
    fast_retention = jax.random.uniform(random_keys[2], (LINE_PIECES, CORE), jnp.float32, 0.85, 0.9)
    retention = jnp.where(slow_segment_mask[None, :], slow_retention * surge_factor[:, None], fast_retention)
    return retention / scale[None, :]


def touch_ends(array, stream_key, low, high):
    longest = array.shape.index(max(array.shape))
    spots = []
    for shift in (0, 1):
        where = [jax.random.randint(jax.random.fold_in(stream_key, axis), (), 0, length) for axis, length in enumerate(array.shape)]
        where[longest] = (where[longest] + shift) % array.shape[longest]
        spots.append(tuple(where))
    return array.at[spots[0]].set(low).at[spots[1]].set(high)


def steps_of(key, extent, pieces, low, largest):
    def one(dim, parts):
        heights = jax.random.uniform(jax.random.fold_in(jax.random.fold_in(key, 6), dim), (parts,), jnp.float32, low / len(pieces), largest / len(pieces))
        return jnp.repeat(jnp.exp(heights), extent[dim] // parts).reshape((-1,) + (1,) * (len(extent) - dim - 1))

    factor_of = one(*pieces[0])
    for cut in pieces[1:]:
        factor_of = factor_of * one(*cut)
    return factor_of


def normal_values(key, dims, deviation, reach, cuts=(), kind=jnp.bfloat16):
    level = steps_of(key, dims, cuts, -0.22, 0.18) if cuts else 1.0
    entries = jax.random.normal(key, dims, jnp.float32) * deviation * level
    return jnp.minimum(jnp.maximum(entries, -reach), reach).astype(kind)


def setup_inputs(seed: int = 0) -> dict:
    keys = jax.random.split(jax.random.key(seed), 8)
    return {
        "starting_warming": normal_values(keys[0], (LINE_PIECES, LOAD_CASES, GRID_NODES), 1.0, 6.0, ((0, 16), (1, 2)), jnp.float32),
        "schur_reciprocal": draw_schur_reciprocal(jax.random.fold_in(keys[7], 71), 0),
        "ground_level_group": touch_ends(jax.random.randint(keys[2], (LINE_PIECES,), 0, CLASSES), jax.random.fold_in(keys[2], 1), 0, CLASSES - 1).astype(jnp.int32),
        "link_coefficient": draw_link_coefficient(jax.random.fold_in(keys[7], 71), 0),
        "dissipation_matrices": jnp.clip(jnp.exp(math.log(1.0) - 2.9957323 * jax.random.uniform(keys[4], (N_SCEN, LINE_PIECES, CIRCUITS, GRID_NODES), jnp.float32) ** steps_of(keys[4], (N_SCEN, LINE_PIECES, CIRCUITS, GRID_NODES), ((0, 2), (1, 16)), -0.2, 0.2)), 0.05, 1.0),
        "timestep_holder": touch_ends(jax.random.randint(keys[5], (HOURS, CIRCUITS), 0, N_SCEN), jax.random.fold_in(keys[5], 1), 0, N_SCEN - 1).astype(jnp.int32),
        "current_demand": touch_ends(jax.random.randint(keys[6], (HOURS, CIRCUITS, LOAD_CASES), 0, 11), jax.random.fold_in(keys[6], 1), 0, 10).astype(jnp.int32),
    }


highest = lax.Precision.HIGHEST
clock_timestep = 1.0
level_step = 0.1


def reference(starting_warming, schur_reciprocal, ground_level_group, link_coefficient, dissipation_matrices, timestep_holder, current_demand):
    inverse_low = schur_reciprocal.astype(jnp.bfloat16)
    thermal_excess = starting_warming
    saved_entries = []
    blank_vector = jnp.zeros((LOAD_CASES, CORE), jnp.float32)
    for hour_step in range(HOURS):
        blocks = jnp.stack([lax.dynamic_index_in_dim(dissipation_matrices[:, :, circuit, :], timestep_holder[hour_step, circuit], 0, keepdims=False) for circuit in range(CIRCUITS)], axis=1)
        current = current_demand[hour_step].astype(jnp.float32) * level_step
        power_input = jnp.sum((current * current)[None, :, :, None] * blocks[:, :, None, :], axis=1)
        applied_power = (thermal_excess + clock_timestep * power_input).astype(jnp.bfloat16)

        def forward(running, inputs):
            row_block, depth_class, gain_row = inputs
            inverse = lax.dynamic_index_in_dim(schur_reciprocal, depth_class, 0, keepdims=False)
            low_inverse = lax.dynamic_index_in_dim(inverse_low, depth_class, 0, keepdims=False)
            solved = jnp.dot(row_block, low_inverse, preferred_element_type=jnp.float32)
            solved = solved + jnp.dot(gain_row[None, :] * running, inverse[:CORE], precision=highest)
            return solved[:, :CORE], solved

        discarded_element, lower_solve_lines = lax.scan(forward, blank_vector, (applied_power, ground_level_group, link_coefficient))

        def upper_solve(running, inputs):
            row_block, depth_class, gain_row = inputs
            inverse = lax.dynamic_index_in_dim(schur_reciprocal, depth_class, 0, keepdims=False)
            result = row_block + jnp.dot(running, inverse[:CORE], precision=highest)
            return gain_row[None, :] * result[:, :CORE], result

        discarded_element, thermal_excess = lax.scan(upper_solve, blank_vector, (lower_solve_lines, ground_level_group, link_coefficient), reverse=True)
        saved_entries.append(thermal_excess)
    return jnp.stack(saved_entries)
```

```python
import functools

import jax
import jax.numpy as jnp
from jax import lax
from jax.experimental import pallas as pl
from jax.experimental.pallas import tpu as pltpu
from jax.sharding import PartitionSpec as P

HOURS = 2
GROUP = 4
clock_timestep = 1.0
level_step = 0.1
bf16 = jnp.bfloat16
f32 = jnp.float32
MESH = pl.DeviceIdType.MESH


def split(x):
    high = x.astype(bf16)
    return high, (x - high.astype(f32)).astype(bf16)


def pack(matrix):
    high, low = split(matrix)
    return jnp.concatenate(
        [
            jnp.concatenate([high, low], axis=1),
            jnp.concatenate([high, jnp.zeros_like(low)], axis=1),
        ],
        axis=0,
    )


def mm3(x, tile):
    high = x.astype(bf16).astype(f32)
    both = jnp.concatenate([high, x - high], axis=1).astype(bf16)
    y = jnp.dot(both, tile, preferred_element_type=f32)
    half = y.shape[1] // 2
    return y[:, :half] + y[:, half:]


def mm3_split(x, high_matrix, low_matrix):
    rows = x.shape[0]
    high = x.astype(bf16).astype(f32)
    both = jnp.concatenate([high, x - high], axis=0).astype(bf16)
    y = jnp.dot(both, high_matrix, preferred_element_type=f32)
    return (
        y[:rows]
        + y[rows:]
        + jnp.dot(high.astype(bf16), low_matrix, preferred_element_type=f32)
    )


def kernel(
    n_route,
    n_scen,
    start_ref,
    schur_hbm,
    link_ref,
    class_ref,
    diss_hbm,
    holder_ref,
    square_ref,
    out_ref,
    schur,
    low_stack,
    core_tile,
    row_high,
    row_low,
    links,
    classes,
    class_smem,
    diss,
    tails_out,
    tails,
    carry_out,
    carry_in,
    core_first,
    z_high,
    z_low,
    dev_tile,
    grp_tile,
    part,
    z_local,
    solved_ref,
    schur_sem,
    link_send,
    link_recv,
    class_send,
    class_recv,
    class_sem,
    diss_sem,
    diss_send,
    diss_recv,
    tail_send,
    tail_recv,
    carry_send,
    carry_recv,
):
    segments, cases, nodes = start_ref.shape
    core = link_ref.shape[1]
    class_count = schur.shape[0]
    circuits = diss.shape[2]
    n_groups = n_route // GROUP
    route = lax.axis_index("route")
    scen = lax.axis_index("scen")
    place = lax.rem(route, GROUP)
    group = lax.div(route, GROUP)
    base = group * GROUP

    def mate(k):
        return {"route": base + lax.rem(place + k, GROUP)}

    def other(k):
        return {"scen": lax.rem(scen + k, n_scen)}

    later = {"route": lax.rem(route + GROUP, n_route)}
    former = {"route": lax.rem(route + n_route - GROUP, n_route)}

    core_copy = pltpu.make_async_copy(
        schur_hbm.at[:, pl.ds(0, core), pl.ds(0, core)], core_first, schur_sem.at[0]
    )
    core_copy.start()
    schur_copy = pltpu.make_async_copy(schur_hbm, schur, schur_sem.at[1])
    schur_copy.start()
    own_diss = pltpu.make_async_copy(diss_hbm.at[0], diss.at[scen], diss_sem)
    own_diss.start()

    barrier = pltpu.get_barrier_semaphore()
    for k in range(1, GROUP):
        pl.semaphore_signal(barrier, inc=1, device_id=mate(k), device_id_type=MESH)
    for k in range(1, n_scen):
        pl.semaphore_signal(barrier, inc=1, device_id=other(k), device_id_type=MESH)
    pl.semaphore_signal(barrier, inc=1, device_id=later, device_id_type=MESH)
    pl.semaphore_signal(barrier, inc=1, device_id=former, device_id_type=MESH)
    pl.semaphore_wait(barrier, GROUP + n_scen)

    def send(src, dst, send_sem, recv_sem, device):
        return pltpu.make_async_remote_copy(
            src_ref=src,
            dst_ref=dst,
            send_sem=send_sem,
            recv_sem=recv_sem,
            device_id=device,
            device_id_type=MESH,
        )

    link_copies = []
    for k in range(1, GROUP):
        slot = GROUP - k
        link_copies.append(
            send(link_ref, links.at[slot], link_send.at[k], link_recv.at[slot], mate(k))
        )
        link_copies.append(
            send(class_ref, classes.at[slot], class_send.at[k], class_recv.at[slot], mate(k))
        )
    for copy in link_copies:
        copy.start()
    diss_copies = []
    for k in range(1, n_scen):
        diss_copies.append(
            send(
                diss_hbm.at[0],
                diss.at[scen],
                diss_send.at[k],
                diss_recv.at[scen],
                other(k),
            )
        )
    for copy in diss_copies:
        copy.start()

    links[0] = link_ref[...]
    classes[0] = class_ref[...]
    core_copy.wait()
    for c in range(class_count):
        core_tile[c] = pack(core_first[c])
    for copy in link_copies:
        copy.wait()
    class_copy = pltpu.make_async_copy(classes, class_smem, class_sem)
    class_copy.start()
    class_copy.wait()

    rows_at = lax.broadcasted_iota(jnp.int32, (core, core), 0)
    eye = jnp.where(rows_at == lax.broadcasted_iota(jnp.int32, (core, core), 1), 1.0, 0.0)
    scaled = [[None] * segments for _ in range(GROUP)]
    reached = [[None] * segments for _ in range(GROUP)]
    for i in range(segments):
        for j in range(GROUP):
            line = links[j, i : i + 1, :]
            scaled[j][i] = (eye if i == 0 else reached[j][i - 1]) * line
            reached[j][i] = mm3(scaled[j][i], core_tile[class_smem[j, i, 0]])
    from_u = [None] * GROUP
    from_w = [eye] * GROUP
    for i in reversed(range(segments)):
        for j in range(GROUP):
            line = links[j, i : i + 1, :]
            if j == 0:
                first = scaled[j][i] if from_u[j] is None else scaled[j][i] + from_u[j]
                response = jnp.concatenate([first, from_w[j]], axis=0)
                high, low = split(response)
                z_high[:, i * core : (i + 1) * core] = high
                z_low[:, i * core : (i + 1) * core] = low
            tile = core_tile[class_smem[j, i, 0]]
            if from_u[j] is None:
                from_u[j] = reached[j][i] * line
                from_w[j] = mm3(from_w[j], tile) * line
            else:
                both = mm3(jnp.concatenate([from_u[j], from_w[j]], axis=0), tile)
                from_u[j] = (reached[j][i] + both[:core]) * line
                from_w[j] = both[core:] * line
    for j in range(GROUP):
        dev_tile[j, 0] = pack(reached[j][segments - 1])
        dev_tile[j, 1] = pack(from_u[j])
        dev_tile[j, 2] = pack(from_w[j])

    def slot_of(j):
        return lax.rem(j - place + GROUP, GROUP)

    u = eye
    us = []
    mine = jnp.zeros((core, core), f32)
    for j in range(GROUP):
        us.append(u)
        mine = jnp.where(place == j, u, mine)
        u = mm3(u, dev_tile[slot_of(j), 0])
    grp_tile[0] = pack(u)
    grp_tile[3] = pack(mine)
    wu = jnp.zeros((core, core), f32)
    ww = eye
    mine_u = jnp.zeros((core, core), f32)
    mine_w = jnp.zeros((core, core), f32)
    for j in reversed(range(GROUP)):
        mine_u = jnp.where(place == j, wu, mine_u)
        mine_w = jnp.where(place == j, ww, mine_w)
        both = mm3(jnp.concatenate([wu, ww], axis=0), dev_tile[slot_of(j), 2])
        wu = both[:core] + mm3(us[j], dev_tile[slot_of(j), 1])
        ww = both[core:]
    grp_tile[1] = pack(wu)
    grp_tile[2] = pack(ww)
    grp_tile[4] = pack(mine_u)
    grp_tile[5] = pack(mine_w)

    schur_copy.wait()
    for c in range(class_count):
        low_stack[c * nodes : (c + 1) * nodes, :] = schur[c].astype(bf16)
        high, low = split(schur[c, :core, :])
        row_high[c * core : (c + 1) * core, :] = high
        row_low[c * core : (c + 1) * core, :] = low
    own_diss.wait()
    for copy in diss_copies:
        copy.wait_send()
    for k in range(1, n_scen):
        source = lax.rem(scen + k, n_scen)
        send(
            diss_hbm.at[0], diss.at[source], diss_send.at[k], diss_recv.at[source], other(k)
        ).wait_recv()

    count = segments * cases
    row_class = jnp.broadcast_to(
        class_ref[...][:, None, :], (segments, cases, core)
    ).reshape(count, core)[:, :1]

    def by_class(x):
        return jnp.concatenate(
            [jnp.where(row_class == c, x, 0.0) for c in range(class_count)], axis=1
        )

    tail_sends = []
    for hour in range(HOURS):
        before = start_ref[...] if hour == 0 else out_ref[hour - 1]
        squares = square_ref[hour]
        power = None
        for c in range(circuits):
            block = diss[holder_ref[hour, c], :, c, :]
            term = squares[:, c : c + 1][None] * block[:, None, :]
            power = term if power is None else power + term
        driving = (before + clock_timestep * power).reshape(count, nodes)
        driving = driving.astype(bf16).astype(f32)
        solved = jnp.dot(
            by_class(driving).astype(bf16), low_stack[...], preferred_element_type=f32
        )
        solved_ref[...] = solved

        u = None
        entering = []
        reach = []
        for i in range(segments):
            line = link_ref[i : i + 1, :]
            own = solved[i * cases : (i + 1) * cases, :core]
            if u is None:
                entering.append(None)
                u = own
            else:
                entering.append(u * line)
                u = own + mm3(entering[i], core_tile[class_smem[0, i, 0]])
            reach.append(u)
        w = None
        for i in reversed(range(segments)):
            line = link_ref[i : i + 1, :]
            if w is None:
                z_local[i] = entering[i] if entering[i] is not None else jnp.zeros_like(u)
                w = reach[i] * line
            else:
                z_local[i] = w if entering[i] is None else entering[i] + w
                w = (reach[i] + mm3(w, core_tile[class_smem[0, i, 0]])) * line
        tails[hour, 0] = jnp.concatenate([u, w], axis=0)
        tails_out[hour] = jnp.concatenate([u, w], axis=0)
        copies = []
        for k in range(1, GROUP):
            slot = GROUP - k
            copies.append(
                send(
                    tails_out.at[hour],
                    tails.at[hour, slot],
                    tail_send.at[hour, k],
                    tail_recv.at[hour, slot],
                    mate(k),
                )
            )
        for copy in copies:
            copy.start()
        for copy in copies:
            copy.wait()

        u = jnp.zeros((cases, core), f32)
        u_mine = jnp.zeros((cases, core), f32)
        us = []
        for j in range(GROUP):
            slot = slot_of(j)
            us.append(u)
            u_mine = jnp.where(place == j, u, u_mine)
            own = tails[hour, slot, :cases]
            u = own if j == 0 else own + mm3(u, dev_tile[slot, 0])
        w = jnp.zeros((cases, core), f32)
        w_mine = jnp.zeros((cases, core), f32)
        for j in reversed(range(GROUP)):
            slot = slot_of(j)
            w_mine = jnp.where(place == j, w, w_mine)
            own = tails[hour, slot, cases:]
            if j > 0:
                own = own + mm3(us[j], dev_tile[slot, 1])
            w = own if j == GROUP - 1 else own + mm3(w, dev_tile[slot, 2])

        forward_send = send(
            carry_out.at[hour, 0],
            carry_in.at[hour, 0],
            carry_send.at[hour, 0],
            carry_recv.at[hour, 0],
            later,
        )
        backward_send = send(
            carry_out.at[hour, 1],
            carry_in.at[hour, 1],
            carry_send.at[hour, 1],
            carry_recv.at[hour, 1],
            former,
        )

        @pl.when(group == 0)
        def _():
            carry_in[hour, 0] = jnp.zeros((cases, core), f32)

        @pl.when(group > 0)
        def _():
            forward_send.wait_recv()

        u_in = carry_in[hour, 0]
        carry_out[hour, 0] = u + mm3(u_in, grp_tile[0])

        @pl.when(group < n_groups - 1)
        def _():
            forward_send.start()

        w = w + mm3(u_in, grp_tile[1])
        u_mine = u_mine + mm3(u_in, grp_tile[3])
        w_mine = w_mine + mm3(u_in, grp_tile[4])

        @pl.when(group == n_groups - 1)
        def _():
            carry_in[hour, 1] = jnp.zeros((cases, core), f32)

        @pl.when(group < n_groups - 1)
        def _():
            backward_send.wait_recv()

        w_in = carry_in[hour, 1]
        carry_out[hour, 1] = w + mm3(w_in, grp_tile[2])

        @pl.when(group > 0)
        def _():
            backward_send.start()

        w_mine = w_mine + mm3(w_in, grp_tile[5])
        spread = mm3_split(
            jnp.concatenate([u_mine, w_mine], axis=1), z_high[...], z_low[...]
        )
        z = jnp.concatenate(
            [z_local[i] + spread[:, i * core : (i + 1) * core] for i in range(segments)],
            axis=0,
        )
        result = solved_ref[...] + mm3_split(by_class(z), row_high[...], row_low[...])
        out_ref[hour] = result.reshape(segments, cases, nodes)

        @pl.when(group < n_groups - 1)
        def _():
            forward_send.wait_send()

        @pl.when(group > 0)
        def _():
            backward_send.wait_send()


def shards(start, schur, groups, link, diss, holder, demand):
    segments, cases, nodes = start.shape
    core = link.shape[1]
    class_count = schur.shape[0]
    circuits = diss.shape[2]
    n_route = lax.axis_size("route")
    n_scen = lax.axis_size("scen")
    current = demand.astype(f32) * level_step
    squares = jnp.transpose(current * current, (0, 2, 1))
    class_rows = jnp.broadcast_to(groups[:, None], (segments, core))
    vmem = pl.BlockSpec(memory_space=pltpu.VMEM)
    hbm = pl.BlockSpec(memory_space=pl.ANY)
    smem = pl.BlockSpec(memory_space=pltpu.SMEM)
    dma = pltpu.SemaphoreType.DMA
    return pl.pallas_call(
        functools.partial(kernel, n_route, n_scen),
        out_shape=jax.ShapeDtypeStruct((HOURS, segments, cases, nodes), f32),
        in_specs=[vmem, hbm, vmem, vmem, hbm, smem, vmem],
        out_specs=vmem,
        scratch_shapes=[
            pltpu.VMEM((class_count, nodes, nodes), f32),
            pltpu.VMEM((class_count * nodes, nodes), bf16),
            pltpu.VMEM((class_count, 2 * core, 2 * core), bf16),
            pltpu.VMEM((class_count * core, nodes), bf16),
            pltpu.VMEM((class_count * core, nodes), bf16),
            pltpu.VMEM((GROUP, segments, core), f32),
            pltpu.VMEM((GROUP, segments, core), jnp.int32),
            pltpu.SMEM((GROUP, segments, core), jnp.int32),
            pltpu.VMEM((n_scen, segments, circuits, nodes), f32),
            pltpu.VMEM((HOURS, 2 * cases, core), f32),
            pltpu.VMEM((HOURS, GROUP, 2 * cases, core), f32),
            pltpu.VMEM((HOURS, 2, cases, core), f32),
            pltpu.VMEM((HOURS, 2, cases, core), f32),
            pltpu.VMEM((class_count, core, core), f32),
            pltpu.VMEM((2 * core, segments * core), bf16),
            pltpu.VMEM((2 * core, segments * core), bf16),
            pltpu.VMEM((GROUP, 3, 2 * core, 2 * core), bf16),
            pltpu.VMEM((6, 2 * core, 2 * core), bf16),
            pltpu.VMEM((2, cases, core), f32),
            pltpu.VMEM((segments, cases, core), f32),
            pltpu.VMEM((segments * cases, nodes), f32),
            dma((2,)),
            dma((GROUP,)),
            dma((GROUP,)),
            dma((GROUP,)),
            dma((GROUP,)),
            dma,
            dma,
            dma((n_scen,)),
            dma((n_scen,)),
            dma((HOURS, GROUP)),
            dma((HOURS, GROUP)),
            dma((HOURS, 2)),
            dma((HOURS, 2)),
        ],
        compiler_params=pltpu.CompilerParams(
            collective_id=0, has_side_effects=True, vmem_limit_bytes=40 * 1024 * 1024
        ),
    )(start, schur, link, class_rows, diss, holder, squares)


def solution(mesh):
    return jax.shard_map(
        shards,
        mesh=mesh,
        in_specs=(
            P("route", "scen", None),
            P(),
            P("route"),
            P("route", None),
            P("scen", "route", None, None),
            P(),
            P(None, None, "scen"),
        ),
        out_specs=P(None, "route", "scen", None),
        check_vma=False,
    )
```

```python
import functools

import jax
import jax.numpy as jnp
from jax import lax
from jax.experimental import pallas as pl
from jax.experimental.pallas import tpu as pltpu
from jax.sharding import PartitionSpec as P

HOURS = 2
SUB = 4
clock_timestep = 1.0
level_step = 0.1
bf16 = jnp.bfloat16
f32 = jnp.float32
MESH = pl.DeviceIdType.MESH


def split(x):
    high = x.astype(bf16)
    return high, (x - high.astype(f32)).astype(bf16)


def pack(matrix):
    high, low = split(matrix)
    return jnp.concatenate(
        [
            jnp.concatenate([high, low], axis=1),
            jnp.concatenate([high, jnp.zeros_like(low)], axis=1),
        ],
        axis=0,
    )


def mm3(x, tile):
    high = x.astype(bf16).astype(f32)
    both = jnp.concatenate([high, x - high], axis=1).astype(bf16)
    y = jnp.dot(both, tile, preferred_element_type=f32)
    half = y.shape[1] // 2
    return y[:, :half] + y[:, half:]


def mm3_split(x, high_matrix, low_matrix):
    rows = x.shape[0]
    high = x.astype(bf16).astype(f32)
    both = jnp.concatenate([high, x - high], axis=0).astype(bf16)
    y = jnp.dot(both, high_matrix, preferred_element_type=f32)
    return (
        y[:rows]
        + y[rows:]
        + jnp.dot(high.astype(bf16), low_matrix, preferred_element_type=f32)
    )


def kernel(
    n_route,
    n_scen,
    start_hbm,
    schur_hbm,
    link_hbm,
    class_hbm,
    diss_hbm,
    holder_hbm,
    demand_hbm,
    out_ref,
    start_ref,
    schur,
    low_stack,
    core_tile,
    row_high,
    row_low,
    links,
    classes,
    class_smem,
    holder_ref,
    demand,
    diss,
    tails_out,
    tails,
    core_first,
    z_high,
    z_low,
    dev_mat,
    dev_tile,
    sub_tile,
    own_tile,
    z_local,
    solved_ref,
    local_sem,
    link_send,
    link_recv,
    class_send,
    class_recv,
    diss_send,
    diss_recv,
    mat_send,
    mat_recv,
    tail_send,
    tail_recv,
):
    segments, cases, nodes = start_ref.shape
    core = links.shape[2]
    class_count = schur.shape[0]
    circuits = diss.shape[1]
    share = n_route // n_scen
    n_sub = n_route // SUB
    route = lax.axis_index("route")
    scen = lax.axis_index("scen")

    def mate(k):
        return {"route": lax.rem(route + k, n_route)}

    def other(k):
        return {"scen": lax.rem(scen + k, n_scen)}

    def local(src, dst, index):
        copy = pltpu.make_async_copy(src, dst, local_sem.at[index])
        copy.start()
        return copy

    core_copy = local(schur_hbm.at[:, pl.ds(0, core), pl.ds(0, core)], core_first, 0)
    link_copy = local(link_hbm, links.at[route], 1)
    class_copy = local(class_hbm, classes.at[route], 2)
    own_class_copy = local(class_hbm, class_smem.at[route], 3)
    schur_copy = local(schur_hbm, schur, 4)
    start_copy = local(start_hbm, start_ref, 5)
    holder_copy = local(holder_hbm, holder_ref, 6)
    demand_copy = local(demand_hbm, demand, 7)
    own_diss = local(diss_hbm.at[0], diss.at[scen], 8)

    barrier = pltpu.get_barrier_semaphore()
    for k in range(1, n_scen):
        pl.semaphore_signal(barrier, inc=1, device_id=other(k), device_id_type=MESH)
    for k in range(1, n_route):
        pl.semaphore_signal(barrier, inc=1, device_id=mate(k), device_id_type=MESH)
    pl.semaphore_wait(barrier, n_route + n_scen - 2)

    def send(src, dst, send_sem, recv_sem, device):
        return pltpu.make_async_remote_copy(
            src_ref=src,
            dst_ref=dst,
            send_sem=send_sem,
            recv_sem=recv_sem,
            device_id=device,
            device_id_type=MESH,
        )

    def diss_send_to(k, source):
        return send(
            diss_hbm.at[0], diss.at[source], diss_send.at[k], diss_recv.at[source], other(k)
        )

    def link_send_to(k, source):
        return send(
            link_hbm, links.at[source], link_send.at[k], link_recv.at[source], mate(k)
        )

    def class_send_to(k, source):
        return send(
            class_hbm, classes.at[source], class_send.at[k], class_recv.at[source], mate(k)
        )

    def tail_send_to(hour, k, source):
        return send(
            tails_out.at[hour],
            tails.at[hour, source],
            tail_send.at[hour, k],
            tail_recv.at[hour, source],
            mate(k),
        )

    for k in range(1, n_scen):
        diss_send_to(k, scen).start()
    for k in range(1, n_route):
        link_send_to(k, route).start()
        class_send_to(k, route).start()

    core_copy.wait()
    for c in range(class_count):
        core_tile[c] = pack(core_first[c])
    schur_copy.wait()
    for c in range(class_count):
        low_stack[c * nodes : (c + 1) * nodes, :] = schur[c].astype(bf16)
        high, low = split(schur[c, :core, :])
        row_high[c * core : (c + 1) * core, :] = high
        row_low[c * core : (c + 1) * core, :] = low
    link_copy.wait()
    class_copy.wait()
    own_class_copy.wait()
    start_copy.wait()
    holder_copy.wait()
    demand_copy.wait()
    own_diss.wait()

    count = segments * cases
    row_class = jnp.broadcast_to(
        classes[route][:, None, :], (segments, cases, core)
    ).reshape(count, core)[:, :1]

    def by_class(x):
        return jnp.concatenate(
            [jnp.where(row_class == c, x, 0.0) for c in range(class_count)], axis=1
        )

    levels = demand[...].astype(f32) * level_step
    squares = levels * levels
    on_diagonal = lax.broadcasted_iota(
        jnp.int32, (cases, cases), 0
    ) == lax.broadcasted_iota(jnp.int32, (cases, cases), 1)

    def local_part(hour, before):
        power = None
        for c in range(circuits):
            row = jnp.broadcast_to(squares[c, hour : hour + 1, :], (cases, cases))
            factor = jnp.sum(jnp.where(on_diagonal, row, 0.0), axis=1, keepdims=True)
            block = diss[holder_ref[hour, c], c]
            term = factor[None] * block[:, None, :]
            power = term if power is None else power + term
        driving = (before + clock_timestep * power).reshape(count, nodes)
        driving = driving.astype(bf16).astype(f32)
        solved = jnp.dot(
            by_class(driving).astype(bf16), low_stack[...], preferred_element_type=f32
        )
        solved_ref[...] = solved
        u = None
        entering = []
        reach = []
        for i in range(segments):
            line = links[route, i : i + 1, :]
            own = solved[i * cases : (i + 1) * cases, :core]
            if u is None:
                entering.append(None)
                u = own
            else:
                entering.append(u * line)
                u = own + mm3(entering[i], core_tile[class_smem[route, i, 0]])
            reach.append(u)
        w = None
        for i in reversed(range(segments)):
            line = links[route, i : i + 1, :]
            if w is None:
                z_local[i] = entering[i] if entering[i] is not None else jnp.zeros_like(u)
                w = reach[i] * line
            else:
                z_local[i] = w if entering[i] is None else entering[i] + w
                w = (reach[i] + mm3(w, core_tile[class_smem[route, i, 0]])) * line
        tails_out[hour] = jnp.concatenate([u, w], axis=0)
        for k in range(1, n_route):
            tail_send_to(hour, k, route).start()
        tails[hour, route] = jnp.concatenate([u, w], axis=0)

    rows_at = lax.broadcasted_iota(jnp.int32, (core, core), 0)
    eye = jnp.where(rows_at == lax.broadcasted_iota(jnp.int32, (core, core), 1), 1.0, 0.0)

    def transfer(devices, keep):
        chains = range(len(devices))
        scaled = [[None] * segments for _ in chains]
        reached = [[None] * segments for _ in chains]
        for i in range(segments):
            for j in chains:
                line = links[devices[j], i : i + 1, :]
                scaled[j][i] = (eye if i == 0 else reached[j][i - 1]) * line
                reached[j][i] = mm3(
                    scaled[j][i], core_tile[class_smem[devices[j], i, 0]]
                )
        from_u = [None] * len(devices)
        from_w = [eye] * len(devices)
        for i in reversed(range(segments)):
            for j in chains:
                line = links[devices[j], i : i + 1, :]
                if j == 0 and keep:
                    first = (
                        scaled[j][i] if from_u[j] is None else scaled[j][i] + from_u[j]
                    )
                    response = jnp.concatenate([first, from_w[j]], axis=0)
                    high, low = split(response)
                    z_high[:, i * core : (i + 1) * core] = high
                    z_low[:, i * core : (i + 1) * core] = low
                    if i == 0:
                        continue
                tile = core_tile[class_smem[devices[j], i, 0]]
                if from_u[j] is None:
                    from_u[j] = reached[j][i] * line
                    from_w[j] = mm3(from_w[j], tile) * line
                else:
                    both = mm3(jnp.concatenate([from_u[j], from_w[j]], axis=0), tile)
                    from_u[j] = (reached[j][i] + both[:core]) * line
                    from_w[j] = both[core:] * line
        return [(reached[j][segments - 1], from_u[j], from_w[j]) for j in chains]

    for k in range(1, n_scen):
        diss_send_to(k, scen).wait_send()
        diss_send_to(k, lax.rem(scen + k, n_scen)).wait_recv()

    local_part(0, start_ref[...])

    for k in range(1, n_route):
        source = lax.rem(route + k, n_route)
        link_send_to(k, route).wait_send()
        class_send_to(k, route).wait_send()
        link_send_to(k, source).wait_recv()
        class_send_to(k, source).wait_recv()
    all_class_copy = pltpu.make_async_copy(classes, class_smem, local_sem.at[2])
    all_class_copy.start()
    all_class_copy.wait()

    def mat_send_to(k, source):
        part = pl.ds(source * share, share)
        return send(
            dev_mat.at[part], dev_mat.at[part], mat_send.at[k], mat_recv.at[source], other(k)
        )

    devices = [scen * share + j for j in range(share)]
    made = transfer(devices, False)
    for j in range(share):
        for m in range(3):
            dev_mat[devices[j], m] = made[j][m]
    for k in range(1, n_scen):
        mat_send_to(k, scen).start()
    transfer([route], True)
    for j in range(share):
        for m in range(3):
            dev_tile[devices[j], m] = pack(dev_mat[devices[j], m])
    for k in range(1, n_scen):
        source = lax.rem(scen + k, n_scen)
        mat_send_to(k, source).wait_recv()
        for j in range(share):
            for m in range(3):
                dev_tile[source * share + j, m] = pack(dev_mat[source * share + j, m])
    for k in range(1, n_scen):
        mat_send_to(k, scen).wait_send()

    mine = [jnp.zeros((core, core), f32)] * 3
    us = [[eye] for _ in range(n_sub)]
    for j in range(SUB):
        for q in range(n_sub):
            d = q * SUB + j
            u = us[q][j]
            mine[0] = jnp.where(route == d, u, mine[0])
            us[q].append(dev_mat[d, 0] if j == 0 else mm3(u, dev_tile[d, 0]))
    for q in range(n_sub):
        sub_tile[q, 0] = pack(us[q][SUB])
    wu = [jnp.zeros((core, core), f32)] * n_sub
    ww = [eye] * n_sub
    for j in reversed(range(SUB)):
        for q in range(n_sub):
            d = q * SUB + j
            mine[1] = jnp.where(route == d, wu[q], mine[1])
            mine[2] = jnp.where(route == d, ww[q], mine[2])
            turn = dev_mat[d, 1] if j == 0 else mm3(us[q][j], dev_tile[d, 1])
            if j == SUB - 1:
                wu[q] = turn
                ww[q] = dev_mat[d, 2]
            else:
                both = mm3(jnp.concatenate([wu[q], ww[q]], axis=0), dev_tile[d, 2])
                wu[q] = both[:core] + turn
                ww[q] = both[core:]
    for q in range(n_sub):
        sub_tile[q, 1] = pack(wu[q])
        sub_tile[q, 2] = pack(ww[q])
    for m in range(3):
        own_tile[m] = pack(mine[m])

    zero = jnp.zeros((cases, core), f32)

    def finish(hour):
        for k in range(1, n_route):
            tail_send_to(hour, k, route).wait_send()
            tail_send_to(hour, k, lax.rem(route + k, n_route)).wait_recv()
        u_mine = zero
        us = [[zero] for _ in range(n_sub)]
        for j in range(SUB):
            for q in range(n_sub):
                d = q * SUB + j
                u = us[q][j]
                u_mine = jnp.where(route == d, u, u_mine)
                own = tails[hour, d, :cases]
                us[q].append(own if j == 0 else own + mm3(u, dev_tile[d, 0]))
        w_mine = zero
        ws = [zero] * n_sub
        for j in reversed(range(SUB)):
            for q in range(n_sub):
                d = q * SUB + j
                w_mine = jnp.where(route == d, ws[q], w_mine)
                own = tails[hour, d, cases:]
                if j > 0:
                    own = own + mm3(us[q][j], dev_tile[d, 1])
                ws[q] = own if j == SUB - 1 else own + mm3(ws[q], dev_tile[d, 2])
        run = lax.div(route, SUB)
        u = zero
        u_run = zero
        w_run = zero
        ends = []
        for q in range(n_sub):
            u_run = jnp.where(run == q, u, u_run)
            ends.append(ws[q] if q == 0 else ws[q] + mm3(u, sub_tile[q, 1]))
            u = us[q][SUB] if q == 0 else us[q][SUB] + mm3(u, sub_tile[q, 0])
        w = zero
        for q in reversed(range(n_sub)):
            w_run = jnp.where(run == q, w, w_run)
            w = ends[q] if q == n_sub - 1 else ends[q] + mm3(w, sub_tile[q, 2])
        u_mine = u_mine + mm3(u_run, own_tile[0])
        w_mine = w_mine + mm3(u_run, own_tile[1]) + mm3(w_run, own_tile[2])
        spread = mm3_split(
            jnp.concatenate([u_mine, w_mine], axis=1), z_high[...], z_low[...]
        )
        z = jnp.concatenate(
            [z_local[i] + spread[:, i * core : (i + 1) * core] for i in range(segments)],
            axis=0,
        )
        result = solved_ref[...] + mm3_split(by_class(z), row_high[...], row_low[...])
        result = result.reshape(segments, cases, nodes)
        out_ref[hour] = result
        return result

    result = finish(0)
    for hour in range(1, HOURS):
        local_part(hour, result)
        result = finish(hour)


def shards(start, schur, groups, link, diss, holder, demand):
    segments, cases, nodes = start.shape
    core = link.shape[1]
    class_count = schur.shape[0]
    circuits = diss.shape[2]
    n_route = lax.axis_size("route")
    n_scen = lax.axis_size("scen")
    class_rows = jnp.broadcast_to(groups[:, None], (segments, core))
    by_circuit = jnp.transpose(diss, (0, 2, 1, 3))
    demand = jnp.transpose(demand, (1, 0, 2))
    hbm = pl.BlockSpec(memory_space=pltpu.HBM)
    dma = pltpu.SemaphoreType.DMA
    mebibytes = 62
    return pl.pallas_call(
        functools.partial(kernel, n_route, n_scen),
        out_shape=jax.ShapeDtypeStruct((HOURS, segments, cases, nodes), f32),
        in_specs=[hbm] * 7,
        out_specs=pl.BlockSpec(memory_space=pltpu.VMEM),
        scratch_shapes=[
            pltpu.VMEM((segments, cases, nodes), f32),
            pltpu.VMEM((class_count, nodes, nodes), f32),
            pltpu.VMEM((class_count * nodes, nodes), bf16),
            pltpu.VMEM((class_count, 2 * core, 2 * core), bf16),
            pltpu.VMEM((class_count * core, nodes), bf16),
            pltpu.VMEM((class_count * core, nodes), bf16),
            pltpu.VMEM((n_route, segments, core), f32),
            pltpu.VMEM((n_route, segments, core), jnp.int32),
            pltpu.SMEM((n_route, segments, core), jnp.int32),
            pltpu.SMEM(holder.shape, jnp.int32),
            pltpu.VMEM(demand.shape, jnp.int32),
            pltpu.VMEM((n_scen, circuits, segments, nodes), f32),
            pltpu.VMEM((HOURS, 2 * cases, core), f32),
            pltpu.VMEM((HOURS, n_route, 2 * cases, core), f32),
            pltpu.VMEM((class_count, core, core), f32),
            pltpu.VMEM((2 * core, segments * core), bf16),
            pltpu.VMEM((2 * core, segments * core), bf16),
            pltpu.VMEM((n_route, 3, core, core), f32),
            pltpu.VMEM((n_route, 3, 2 * core, 2 * core), bf16),
            pltpu.VMEM((n_route // SUB, 3, 2 * core, 2 * core), bf16),
            pltpu.VMEM((3, 2 * core, 2 * core), bf16),
            pltpu.VMEM((segments, cases, core), f32),
            pltpu.VMEM((segments * cases, nodes), f32),
            dma((9,)),
            dma((n_route,)),
            dma((n_route,)),
            dma((n_route,)),
            dma((n_route,)),
            dma((n_scen,)),
            dma((n_scen,)),
            dma((n_scen,)),
            dma((n_scen,)),
            dma((HOURS, n_route)),
            dma((HOURS, n_route)),
        ],
        compiler_params=pltpu.CompilerParams(
            collective_id=0,
            has_side_effects=True,
            vmem_limit_bytes=mebibytes * 1024 * 1024,
        ),
    )(start, schur, link, class_rows, by_circuit, holder, demand)


def solution(mesh):
    return jax.shard_map(
        shards,
        mesh=mesh,
        in_specs=(
            P("route", "scen", None),
            P(),
            P("route"),
            P("route", None),
            P("scen", "route", None, None),
            P(),
            P(None, None, "scen"),
        ),
        out_specs=P(None, "route", "scen", None),
        check_vma=False,
    )
```

```python
import functools

import jax
import jax.numpy as jnp
from jax import lax
from jax.experimental import pallas as pl
from jax.experimental.pallas import tpu as pltpu
from jax.sharding import PartitionSpec as P

HOURS = 2
SUB = 4
clock_timestep = 1.0
level_step = 0.1
bf16 = jnp.bfloat16
f32 = jnp.float32
MESH = pl.DeviceIdType.MESH


def split(x):
    high = x.astype(bf16)
    return high, (x - high.astype(f32)).astype(bf16)


def pack(matrix):
    high, low = split(matrix)
    return jnp.concatenate(
        [
            jnp.concatenate([high, low], axis=1),
            jnp.concatenate([high, jnp.zeros_like(low)], axis=1),
        ],
        axis=0,
    )


def mm3(x, tile):
    high = x.astype(bf16).astype(f32)
    both = jnp.concatenate([high, x - high], axis=1).astype(bf16)
    y = jnp.dot(both, tile, preferred_element_type=f32)
    half = y.shape[1] // 2
    return y[:, :half] + y[:, half:]


def mm3_split(x, high_matrix, low_matrix):
    rows = x.shape[0]
    high = x.astype(bf16).astype(f32)
    both = jnp.concatenate([high, x - high], axis=0).astype(bf16)
    y = jnp.dot(both, high_matrix, preferred_element_type=f32)
    return (
        y[:rows]
        + y[rows:]
        + jnp.dot(high.astype(bf16), low_matrix, preferred_element_type=f32)
    )


def kernel(
    n_route,
    n_scen,
    start_hbm,
    schur_hbm,
    link_hbm,
    class_hbm,
    diss_hbm,
    holder_hbm,
    demand_hbm,
    out_ref,
    start_ref,
    schur,
    low_stack,
    core_tile,
    row_high,
    row_low,
    links,
    classes,
    class_smem,
    own_class,
    holder_ref,
    demand,
    diss,
    tails_out,
    tails,
    core_first,
    z_high,
    z_low,
    dev_mat,
    dev_tile,
    sub_tile,
    own_tile,
    z_local,
    solved_ref,
    local_sem,
    link_send,
    link_recv,
    class_send,
    class_recv,
    diss_send,
    diss_recv,
    mat_send,
    mat_recv,
    tail_send,
    tail_recv,
):
    segments, cases, nodes = start_ref.shape
    core = links.shape[2]
    class_count = schur.shape[0]
    circuits = diss.shape[1]
    share = n_route // n_scen
    n_sub = n_route // SUB
    route = lax.axis_index("route")
    scen = lax.axis_index("scen")

    def mate(k):
        return {"route": lax.rem(route + k, n_route)}

    def other(k):
        return {"scen": lax.rem(scen + k, n_scen)}

    def local(src, dst, index):
        copy = pltpu.make_async_copy(src, dst, local_sem.at[index])
        copy.start()
        return copy

    core_copy = local(schur_hbm.at[:, pl.ds(0, core), pl.ds(0, core)], core_first, 0)
    link_copy = local(link_hbm, links.at[route], 1)
    own_class_copy = local(class_hbm, own_class, 3)
    schur_copy = local(schur_hbm, schur, 4)
    start_copy = local(start_hbm, start_ref, 5)
    holder_copy = local(holder_hbm, holder_ref, 6)
    demand_copy = local(demand_hbm, demand, 7)
    own_diss = local(diss_hbm.at[0], diss.at[scen], 8)

    barrier = pltpu.get_barrier_semaphore()
    for k in range(1, n_scen):
        pl.semaphore_signal(barrier, inc=1, device_id=other(k), device_id_type=MESH)
    for k in range(1, n_route):
        pl.semaphore_signal(barrier, inc=1, device_id=mate(k), device_id_type=MESH)
    own_class_copy.wait()
    own_classes = [own_class[i] for i in range(segments)]
    for i in range(segments):
        classes[route, i : i + 1, :] = jnp.full((1, core), own_classes[i], jnp.int32)
    pl.semaphore_wait(barrier, n_route + n_scen - 2)

    def send(src, dst, send_sem, recv_sem, device):
        return pltpu.make_async_remote_copy(
            src_ref=src,
            dst_ref=dst,
            send_sem=send_sem,
            recv_sem=recv_sem,
            device_id=device,
            device_id_type=MESH,
        )

    def diss_send_to(k, source):
        return send(
            diss_hbm.at[0], diss.at[source], diss_send.at[k], diss_recv.at[source], other(k)
        )

    def link_send_to(k, source):
        return send(
            link_hbm, links.at[source], link_send.at[k], link_recv.at[source], mate(k)
        )

    def class_send_to(k, source):
        return send(
            classes.at[route], classes.at[source], class_send.at[k], class_recv.at[source], mate(k)
        )

    def tail_send_to(hour, k, source):
        return send(
            tails_out.at[hour],
            tails.at[hour, source],
            tail_send.at[hour, k],
            tail_recv.at[hour, source],
            mate(k),
        )

    for k in range(1, n_scen):
        diss_send_to(k, scen).start()
    for k in range(1, n_route):
        link_send_to(k, route).start()
        class_send_to(k, route).start()

    core_copy.wait()
    for c in range(class_count):
        core_tile[c] = pack(core_first[c])
    schur_copy.wait()
    for c in range(class_count):
        low_stack[c * nodes : (c + 1) * nodes, :] = schur[c].astype(bf16)
        high, low = split(schur[c, :core, :])
        row_high[c * core : (c + 1) * core, :] = high
        row_low[c * core : (c + 1) * core, :] = low
    link_copy.wait()
    start_copy.wait()
    holder_copy.wait()
    demand_copy.wait()
    own_diss.wait()

    count = segments * cases
    row_class = jnp.broadcast_to(
        classes[route][:, None, :], (segments, cases, core)
    ).reshape(count, core)[:, :1]

    def by_class(x):
        return jnp.concatenate(
            [jnp.where(row_class == c, x, 0.0) for c in range(class_count)], axis=1
        )

    levels = demand[...].astype(f32) * level_step
    squares = levels * levels
    on_diagonal = lax.broadcasted_iota(
        jnp.int32, (cases, cases), 0
    ) == lax.broadcasted_iota(jnp.int32, (cases, cases), 1)

    def local_part(hour, before):
        power = None
        for c in range(circuits):
            row = jnp.broadcast_to(squares[c, hour : hour + 1, :], (cases, cases))
            factor = jnp.sum(jnp.where(on_diagonal, row, 0.0), axis=1, keepdims=True)
            block = diss[holder_ref[hour, c], c]
            term = factor[None] * block[:, None, :]
            power = term if power is None else power + term
        driving = (before + clock_timestep * power).reshape(count, nodes)
        driving = driving.astype(bf16).astype(f32)
        solved = jnp.dot(
            by_class(driving).astype(bf16), low_stack[...], preferred_element_type=f32
        )
        solved_ref[...] = solved
        u = None
        entering = []
        reach = []
        for i in range(segments):
            line = links[route, i : i + 1, :]
            own = solved[i * cases : (i + 1) * cases, :core]
            if u is None:
                entering.append(None)
                u = own
            else:
                entering.append(u * line)
                u = own + mm3(entering[i], core_tile[own_classes[i]])
            reach.append(u)
        w = None
        for i in reversed(range(segments)):
            line = links[route, i : i + 1, :]
            if w is None:
                z_local[i] = entering[i] if entering[i] is not None else jnp.zeros_like(u)
                w = reach[i] * line
            else:
                z_local[i] = w if entering[i] is None else entering[i] + w
                w = (reach[i] + mm3(w, core_tile[own_classes[i]])) * line
        tails_out[hour] = jnp.concatenate([u, w], axis=0)
        for k in range(1, n_route):
            tail_send_to(hour, k, route).start()
        tails[hour, route] = jnp.concatenate([u, w], axis=0)

    rows_at = lax.broadcasted_iota(jnp.int32, (core, core), 0)
    eye = jnp.where(rows_at == lax.broadcasted_iota(jnp.int32, (core, core), 1), 1.0, 0.0)

    def transfer(devices, keep):
        chains = range(len(devices))
        scaled = [[None] * segments for _ in chains]
        reached = [[None] * segments for _ in chains]
        for i in range(segments):
            for j in chains:
                line = links[devices[j], i : i + 1, :]
                scaled[j][i] = (eye if i == 0 else reached[j][i - 1]) * line
                reached[j][i] = mm3(
                    scaled[j][i], core_tile[class_smem[devices[j], i, 0]]
                )
        from_u = [None] * len(devices)
        from_w = [eye] * len(devices)
        for i in reversed(range(segments)):
            for j in chains:
                line = links[devices[j], i : i + 1, :]
                if j == 0 and keep:
                    first = (
                        scaled[j][i] if from_u[j] is None else scaled[j][i] + from_u[j]
                    )
                    response = jnp.concatenate([first, from_w[j]], axis=0)
                    high, low = split(response)
                    z_high[:, i * core : (i + 1) * core] = high
                    z_low[:, i * core : (i + 1) * core] = low
                    if i == 0:
                        continue
                tile = core_tile[class_smem[devices[j], i, 0]]
                if from_u[j] is None:
                    from_u[j] = reached[j][i] * line
                    from_w[j] = mm3(from_w[j], tile) * line
                else:
                    both = mm3(jnp.concatenate([from_u[j], from_w[j]], axis=0), tile)
                    from_u[j] = (reached[j][i] + both[:core]) * line
                    from_w[j] = both[core:] * line
        return [(reached[j][segments - 1], from_u[j], from_w[j]) for j in chains]

    for k in range(1, n_scen):
        diss_send_to(k, scen).wait_send()
        diss_send_to(k, lax.rem(scen + k, n_scen)).wait_recv()

    for k in range(1, n_route):
        source = lax.rem(route + k, n_route)
        link_send_to(k, route).wait_send()
        class_send_to(k, route).wait_send()
        link_send_to(k, source).wait_recv()
        class_send_to(k, source).wait_recv()
    all_class_copy = pltpu.make_async_copy(classes, class_smem, local_sem.at[2])
    all_class_copy.start()
    local_part(0, start_ref[...])

    all_class_copy.wait()

    def mat_send_to(k, source):
        part = pl.ds(source * share, share)
        return send(
            dev_mat.at[part], dev_mat.at[part], mat_send.at[k], mat_recv.at[source], other(k)
        )

    devices = [scen * share + j for j in range(share)]
    made = transfer(devices, False)
    for j in range(share):
        for m in range(3):
            dev_mat[devices[j], m] = made[j][m]
    for k in range(1, n_scen):
        mat_send_to(k, scen).start()
    transfer([route], True)
    for j in range(share):
        for m in range(3):
            dev_tile[devices[j], m] = pack(dev_mat[devices[j], m])
    for k in range(1, n_scen):
        source = lax.rem(scen + k, n_scen)
        mat_send_to(k, source).wait_recv()
        for j in range(share):
            for m in range(3):
                dev_tile[source * share + j, m] = pack(dev_mat[source * share + j, m])
    for k in range(1, n_scen):
        mat_send_to(k, scen).wait_send()

    mine = [jnp.zeros((core, core), f32)] * 3
    us = [[eye] for _ in range(n_sub)]
    for j in range(SUB):
        for q in range(n_sub):
            d = q * SUB + j
            u = us[q][j]
            mine[0] = jnp.where(route == d, u, mine[0])
            us[q].append(dev_mat[d, 0] if j == 0 else mm3(u, dev_tile[d, 0]))
    for q in range(n_sub):
        sub_tile[q, 0] = pack(us[q][SUB])
    wu = [jnp.zeros((core, core), f32)] * n_sub
    ww = [eye] * n_sub
    for j in reversed(range(SUB)):
        for q in range(n_sub):
            d = q * SUB + j
            mine[1] = jnp.where(route == d, wu[q], mine[1])
            mine[2] = jnp.where(route == d, ww[q], mine[2])
            turn = dev_mat[d, 1] if j == 0 else mm3(us[q][j], dev_tile[d, 1])
            if j == SUB - 1:
                wu[q] = turn
                ww[q] = dev_mat[d, 2]
            else:
                both = mm3(jnp.concatenate([wu[q], ww[q]], axis=0), dev_tile[d, 2])
                wu[q] = both[:core] + turn
                ww[q] = both[core:]
    for q in range(n_sub):
        sub_tile[q, 1] = pack(wu[q])
        sub_tile[q, 2] = pack(ww[q])
    for m in range(3):
        own_tile[m] = pack(mine[m])

    zero = jnp.zeros((cases, core), f32)

    def finish(hour):
        for k in range(1, n_route):
            tail_send_to(hour, k, route).wait_send()
            tail_send_to(hour, k, lax.rem(route + k, n_route)).wait_recv()
        u_mine = zero
        us = [[zero] for _ in range(n_sub)]
        for j in range(SUB):
            for q in range(n_sub):
                d = q * SUB + j
                u = us[q][j]
                u_mine = jnp.where(route == d, u, u_mine)
                own = tails[hour, d, :cases]
                us[q].append(own if j == 0 else own + mm3(u, dev_tile[d, 0]))
        w_mine = zero
        ws = [zero] * n_sub
        for j in reversed(range(SUB)):
            for q in range(n_sub):
                d = q * SUB + j
                w_mine = jnp.where(route == d, ws[q], w_mine)
                own = tails[hour, d, cases:]
                if j > 0:
                    own = own + mm3(us[q][j], dev_tile[d, 1])
                ws[q] = own if j == SUB - 1 else own + mm3(ws[q], dev_tile[d, 2])
        run = lax.div(route, SUB)
        u = zero
        u_run = zero
        w_run = zero
        ends = []
        for q in range(n_sub):
            u_run = jnp.where(run == q, u, u_run)
            ends.append(ws[q] if q == 0 else ws[q] + mm3(u, sub_tile[q, 1]))
            u = us[q][SUB] if q == 0 else us[q][SUB] + mm3(u, sub_tile[q, 0])
        w = zero
        for q in reversed(range(n_sub)):
            w_run = jnp.where(run == q, w, w_run)
            w = ends[q] if q == n_sub - 1 else ends[q] + mm3(w, sub_tile[q, 2])
        u_mine = u_mine + mm3(u_run, own_tile[0])
        w_mine = w_mine + mm3(u_run, own_tile[1]) + mm3(w_run, own_tile[2])
        spread = mm3_split(
            jnp.concatenate([u_mine, w_mine], axis=1), z_high[...], z_low[...]
        )
        z = jnp.concatenate(
            [z_local[i] + spread[:, i * core : (i + 1) * core] for i in range(segments)],
            axis=0,
        )
        result = solved_ref[...] + mm3_split(by_class(z), row_high[...], row_low[...])
        result = result.reshape(segments, cases, nodes)
        out_ref[hour] = result
        return result

    result = finish(0)
    for hour in range(1, HOURS):
        local_part(hour, result)
        result = finish(hour)


def shards(start, schur, groups, link, diss, holder, demand):
    segments, cases, nodes = start.shape
    core = link.shape[1]
    class_count = schur.shape[0]
    circuits = diss.shape[2]
    n_route = lax.axis_size("route")
    n_scen = lax.axis_size("scen")
    by_circuit = jnp.transpose(diss, (0, 2, 1, 3))
    demand = jnp.transpose(demand, (1, 0, 2))
    hbm = pl.BlockSpec(memory_space=pltpu.HBM)
    dma = pltpu.SemaphoreType.DMA
    mebibytes = 62
    return pl.pallas_call(
        functools.partial(kernel, n_route, n_scen),
        out_shape=jax.ShapeDtypeStruct((HOURS, segments, cases, nodes), f32),
        in_specs=[hbm] * 7,
        out_specs=pl.BlockSpec(memory_space=pltpu.VMEM),
        scratch_shapes=[
            pltpu.VMEM((segments, cases, nodes), f32),
            pltpu.VMEM((class_count, nodes, nodes), f32),
            pltpu.VMEM((class_count * nodes, nodes), bf16),
            pltpu.VMEM((class_count, 2 * core, 2 * core), bf16),
            pltpu.VMEM((class_count * core, nodes), bf16),
            pltpu.VMEM((class_count * core, nodes), bf16),
            pltpu.VMEM((n_route, segments, core), f32),
            pltpu.VMEM((n_route, segments, core), jnp.int32),
            pltpu.SMEM((n_route, segments, core), jnp.int32),
            pltpu.SMEM((segments,), jnp.int32),
            pltpu.SMEM(holder.shape, jnp.int32),
            pltpu.VMEM(demand.shape, jnp.int32),
            pltpu.VMEM((n_scen, circuits, segments, nodes), f32),
            pltpu.VMEM((HOURS, 2 * cases, core), f32),
            pltpu.VMEM((HOURS, n_route, 2 * cases, core), f32),
            pltpu.VMEM((class_count, core, core), f32),
            pltpu.VMEM((2 * core, segments * core), bf16),
            pltpu.VMEM((2 * core, segments * core), bf16),
            pltpu.VMEM((n_route, 3, core, core), f32),
            pltpu.VMEM((n_route, 3, 2 * core, 2 * core), bf16),
            pltpu.VMEM((n_route // SUB, 3, 2 * core, 2 * core), bf16),
            pltpu.VMEM((3, 2 * core, 2 * core), bf16),
            pltpu.VMEM((segments, cases, core), f32),
            pltpu.VMEM((segments * cases, nodes), f32),
            dma((9,)),
            dma((n_route,)),
            dma((n_route,)),
            dma((n_route,)),
            dma((n_route,)),
            dma((n_scen,)),
            dma((n_scen,)),
            dma((n_scen,)),
            dma((n_scen,)),
            dma((HOURS, n_route)),
            dma((HOURS, n_route)),
        ],
        compiler_params=pltpu.CompilerParams(
            collective_id=0,
            has_side_effects=True,
            vmem_limit_bytes=mebibytes * 1024 * 1024,
        ),
    )(start, schur, link, groups, by_circuit, holder, demand)


def solution(mesh):
    return jax.shard_map(
        shards,
        mesh=mesh,
        in_specs=(
            P("route", "scen", None),
            P(),
            P("route"),
            P("route", None),
            P("scen", "route", None, None),
            P(),
            P(None, None, "scen"),
        ),
        out_specs=P(None, "route", "scen", None),
        check_vma=False,
    )
```
